128 devices in a mesh: seq: 8 (over y, core), head: 16 (over x, z).
Axes of the slice: x: 4, y: 4, z: 4, core: 2. Of those that a mesh axis runs over, the one named last changes fastest.
Arguments:
- queries: bfloat16 [16384, 4096], P(('seq', 'head')), may hold values from -60 to 60
- encoded: bfloat16 [128, 128, 896], P('seq'), may hold values from -6 to 6
- w_key: bfloat16 [896, 4096], P(None, 'head'), may hold values from -0.1875 to 0.1875
- w_value: bfloat16 [896, 4096], P(None, 'head'), may hold values from -0.1875 to 0.1875
- shard_ids: int32 [256, 2], P(('seq', 'head')), may hold values from 0 to 7, all different within a row; in each aligned block of 2 rows (0 to 1, 2 to 3, ...) at most 2 rows name the same one
- row_ids: int32 [256, 2], P(('seq', 'head')), may hold values from 0 to 15
- grad_out: bfloat16 [16384, 4096], P(('seq', 'head')), may hold values from -6 to 6
Outputs:
- attended: bfloat16 [16384, 4096], P(('seq', 'head'))
- grad_queries: bfloat16 [16384, 4096], P(('seq', 'head'))
- grad_wkey: float32 [896, 4096], P(None, 'head')
- grad_wvalue: float32 [896, 4096], P(None, 'head')
The draws below stay inside these ranges and needn't reach their ends.
Inputs may be any that keep to these rules, and one draw needn't show every extreme that they name: `shard_ids`: the 2 neighbours of one span come from different shards; the spans of one device take at most 2 neighbours from one shard, and some device takes exactly 2.
All inputs are finite; a program needn't handle non-finite values.
Results may differ from the reference program's by a relative error of at most 0.03.
The reference program's roundings to bfloat16 on the way (of `fetched`, `key_proj`, `prob_round`, `grad_score` and `grad_key`) count: a program that leaves them out, or rounds other values in their place, can miss the bound.
Values may be sent and summed in bfloat16 or wider, within the bound.
No kernel may reach another device: no remote copies, remote signals or barrier semaphores. Data moves between devices by JAX's collectives and lax.ppermute only.
A program may use at most 128 MiB of HBM per device.

```python
import math
import jax
import jax.numpy as jnp
import numpy as np
from jax import lax

HEADS = 32
HEAD_DIM = 128
ENC_WIDTH = 896
SPAN = 64
NEIGHBOURS = 2
NEIGH_TOKENS = 128
TOK_DEV = 128
NB_SHARD = 16
CAP = 2
D = 4096
TOKENS = 16384
SPANS = 256
DB_ROWS = 128
N_SEQ = 8


def draw_queries(key, part):
    key = jax.random.fold_in(key, 11)
    first = jax.random.fold_in(key, 0)
    values = jnp.clip(jax.random.normal(first, (TOKENS, D), jnp.float32), -6.0, 6.0)
    return values.astype(jnp.bfloat16)


def set_ends(entries, stream_key, smallest, high):
    longest = entries.shape.index(max(entries.shape))
    spots = []
    for shift in (0, 1):
        where = [jax.random.randint(jax.random.fold_in(stream_key, axis), (), 0, length) for axis, length in enumerate(entries.shape)]
        where[longest] = (where[longest] + shift) % entries.shape[longest]
        spots.append(tuple(where))
    return entries.at[spots[0]].set(smallest).at[spots[1]].set(high)


def steps_of(key, extent, cuts, low, largest):
    gain = 1.0
    for position, parts in cuts:
        draws = jax.random.uniform(jax.random.fold_in(jax.random.fold_in(key, 6), position), (parts,), jnp.float32, low / len(cuts), largest / len(cuts))
        gain = gain * jnp.repeat(jnp.exp(draws), extent[position] // parts).reshape((-1,) + (1,) * (len(extent) - 1 - position))
    return gain


def cumulative_ranks(number_of, lean):
    weights = [(1 << 20) // math.isqrt(grade ** lean) + 1 for grade in range(1, number_of + 1)]
    scale = 1 + sum(weights) // (1 << 30)
    return np.cumsum(np.array([max(1, weight // scale) for weight in weights]))


def ranked(key, shape, number_of, slope):
    listing = cumulative_ranks(number_of, slope)
    pick = jax.random.randint(jax.random.fold_in(key, 1), shape, 0, int(listing[number_of - 1]))
    grade = jnp.searchsorted(jnp.asarray(listing, jnp.int32), pick, side="right")
    return jax.random.permutation(jax.random.fold_in(key, 2), number_of)[grade].astype(jnp.int32)


def assign_block(rng, own, number, rows, number_of, top, bound, skew):
    ranking = jax.random.permutation(rng, number_of)
    crowded, usual = shares(number_of, rows * top, bound, skew, True), shares(number_of, rows * top, bound, skew, False)
    places = jnp.arange(number_of)

    def named(sizes, turn):
        used = int((sizes > 0).sum())
        fixed = max(1, used // 4)
        shifted = fixed + (places - fixed + turn * (used - fixed)) % max(1, number_of - fixed)
        return jnp.zeros((number_of,), jnp.int32).at[ranking[jnp.where(places < fixed, places, shifted)]].set(jnp.asarray(sizes, jnp.int32))

    sizes = jnp.where(number % 4 == 0, named(crowded, number // 4), named(usual, number - number // 4 - 1))
    mixed = jax.random.permutation(jax.random.fold_in(own, 3), number_of)
    giver, taker = mixed[0:number_of // 2 * 2:2], mixed[1:number_of // 2 * 2:2]
    room = jnp.minimum(sizes[giver] - 1, bound - sizes[taker]) // 2
    room = jnp.where((giver == ranking[0]) | (taker == ranking[0]) | (sizes[taker] == 0), 0, jnp.maximum(room, 0))
    shifted = jax.random.randint(jax.random.fold_in(own, 4), (number_of // 2,), 0, 1 << 20) % (room + 1)
    sizes = sizes.at[giver].add(-shifted).at[taker].add(shifted)
    labels = jnp.searchsorted(jnp.cumsum(sizes), jnp.arange(rows * top), side="right").astype(jnp.int32)
    table = labels.reshape(top, rows).T
    table = table[jax.random.permutation(jax.random.fold_in(own, 1), rows)]
    turn = jax.random.randint(jax.random.fold_in(own, 2), (rows, 1), 0, top)
    return jnp.take_along_axis(table, (jnp.arange(top)[None, :] + turn) % top, axis=1)


def shares(count, total, bound, skew, full):
    weights = [(1 << 20) // math.isqrt(rank ** skew) + 1 for rank in range(1, count + 1)]
    largest = bound if full else min(bound, max(-(-total // count), total * weights[0] // sum(weights)))
    least = 1 if total - largest >= count - 1 else 0
    given, spare = [largest] + [least] * (count - 1), total - largest - least * (count - 1)
    while spare > 0:
        free = [i for i in range(1, count) if given[i] < largest] or [i for i in range(1, count) if given[i] < bound]
        pool, remaining = sum([weights[i] for i in free]), spare
        for i in free:
            addition = min(bound - given[i], max(1, remaining * weights[i] // pool), spare)
            given[i] = given[i] + addition
            spare = spare - addition
    return np.array(given)


def gaussian(rng, dims, deviation, most, cuts=(), dtype=jnp.bfloat16):
    values = deviation * jax.random.normal(rng, dims, jnp.float32)
    if cuts:
        values = values * steps_of(rng, dims, cuts, -0.22, 0.18)
    return jnp.clip(values, -most, most).astype(dtype)


def setup_inputs(seed: int = 0) -> dict:
    key_of = jax.random.split(jax.random.key(seed), 8)
    queries = draw_queries(jax.random.fold_in(key_of[7], 71), 0)
    encoded = gaussian(key_of[1], (DB_ROWS, NEIGH_TOKENS, ENC_WIDTH), 1.0, 6.0, ((0, 8),))
    w_key = gaussian(key_of[2], (ENC_WIDTH, D), ENC_WIDTH ** -0.5, 0.1875, ((1, 16),))
    w_value = gaussian(key_of[3], (ENC_WIDTH, D), ENC_WIDTH ** -0.5, 0.1875, ((1, 16),))
    shard_ids_keys = jax.random.split(jax.random.fold_in(key_of[4], 1), SPANS // (TOK_DEV // SPAN))
    shard_ids_turns = jax.random.permutation(jax.random.fold_in(key_of[4], 3), SPANS // (TOK_DEV // SPAN))
    shard_ids = jax.vmap(lambda own, number: assign_block(jax.random.fold_in(key_of[4], 2), own, number, TOK_DEV // SPAN, N_SEQ, NEIGHBOURS, CAP, 2))(shard_ids_keys, shard_ids_turns).reshape((SPANS, NEIGHBOURS))
    row_ids = set_ends(ranked(key_of[5], (SPANS, NEIGHBOURS), NB_SHARD, 2), jax.random.fold_in(key_of[5], 3), 0, NB_SHARD - 1).astype(jnp.int32)
    grad_out = gaussian(key_of[6], (TOKENS, D), 1.0, 6.0, ((0, 128),))
    return dict(queries=queries, encoded=encoded, w_key=w_key, w_value=w_value, shard_ids=shard_ids, row_ids=row_ids, grad_out=grad_out)


def reference(queries, encoded, w_key, w_value, shard_ids, row_ids, grad_out):
    scale = HEAD_DIM ** -0.5
    query_blocks = queries.reshape(SPANS, SPAN, HEADS, HEAD_DIM)
    grad_blocks = grad_out.reshape(SPANS, SPAN, HEADS, HEAD_DIM)
    row_index = (shard_ids * NB_SHARD + row_ids).astype(jnp.int32)

    def span_step(totals, inputs):
        sum_wkey, sum_wvalue = totals
        query_one, grad_one, index_one = inputs
        fetched = encoded[index_one].reshape(NEIGHBOURS * NEIGH_TOKENS, ENC_WIDTH)
        key_proj = jnp.dot(fetched, w_key, preferred_element_type=jnp.float32).astype(jnp.bfloat16)
        value_proj = jnp.dot(fetched, w_value, preferred_element_type=jnp.float32).astype(jnp.bfloat16)
        key_heads = key_proj.reshape(-1, HEADS, HEAD_DIM).astype(jnp.float32)
        value_heads = value_proj.reshape(-1, HEADS, HEAD_DIM).astype(jnp.float32)
        query_f = query_one.astype(jnp.float32)
        grad_f = grad_one.astype(jnp.float32)
        scores = jnp.einsum('qhd,khd->hqk', query_f, key_heads) * scale
        probability = jax.nn.softmax(scores, axis=-1)
        prob_round = probability.astype(jnp.bfloat16)
        attended = jnp.einsum('hqk,khd->qhd', prob_round.astype(jnp.float32), value_heads).astype(jnp.bfloat16)
        grad_prob = jnp.einsum('qhd,khd->hqk', grad_f, value_heads)
        row_delta = jnp.sum(grad_f * attended.astype(jnp.float32), axis=-1)
        row_delta = jnp.transpose(row_delta)[:, :, None]
        grad_score = (probability * (grad_prob - row_delta)).astype(jnp.bfloat16)
        grad_score_f = grad_score.astype(jnp.float32)
        grad_query = (jnp.einsum('hqk,khd->qhd', grad_score_f, key_heads) * scale).astype(jnp.bfloat16)
        grad_key = (jnp.einsum('hqk,qhd->khd', grad_score_f, query_f) * scale).astype(jnp.bfloat16)
        grad_value = jnp.einsum('hqk,qhd->khd', prob_round.astype(jnp.float32), grad_f).astype(jnp.bfloat16)
        sum_wkey = sum_wkey + jnp.dot(fetched.T, grad_key.reshape(-1, D), preferred_element_type=jnp.float32)
        sum_wvalue = sum_wvalue + jnp.dot(fetched.T, grad_value.reshape(-1, D), preferred_element_type=jnp.float32)
        return (sum_wkey, sum_wvalue), (attended, grad_query)

    zeros_init = jnp.zeros((ENC_WIDTH, D), jnp.float32)
    totals, outputs = lax.scan(span_step, (zeros_init, zeros_init), (query_blocks, grad_blocks, row_index))
    attended = outputs[0].reshape(TOKENS, D)
    grad_queries = outputs[1].reshape(TOKENS, D)
    return attended, grad_queries, totals[0], totals[1]
```

```python
import functools

import jax
import jax.numpy as jnp
from jax import lax
from jax.experimental import pallas as pl
from jax.experimental.pallas import tpu as pltpu
from jax.sharding import PartitionSpec as P

HEAD_DIM = 128
SPANS_STEP = 4
BF16 = jnp.bfloat16
F32 = jnp.float32
NN = (((1,), (0,)), ((), ()))
NT = (((1,), (1,)), ((), ()))


def dot(a, b, dims=NN):
    return lax.dot_general(a, b, dims, preferred_element_type=F32)


def attention_kernel(
    span_len,
    neighbours,
    ids_ref,
    db_ref,
    wk_ref,
    wv_ref,
    q_ref,
    g_ref,
    att_ref,
    gq_ref,
    dwk_ref,
    dwv_ref,
    rows,
    acc_k,
    acc_v,
    gkt,
    gvt,
    sems,
):
    step, steps = pl.program_id(0), pl.num_programs(0)
    slot = lax.rem(step, 2)
    key_tokens = db_ref.shape[1]
    fetched = SPANS_STEP * neighbours
    keys = neighbours * key_tokens
    heads = wk_ref.shape[1] // HEAD_DIM
    scale = HEAD_DIM ** (-0.5)

    def copies(at, into):
        return [
            pltpu.make_async_copy(
                db_ref.at[ids_ref[at * fetched + j]],
                rows.at[into, pl.ds(j * key_tokens, key_tokens)],
                sems.at[into, j],
            )
            for j in range(fetched)
        ]

    @pl.when(step == 0)
    def _():
        for copy in copies(step, slot):
            copy.start()
        acc_k[...] = jnp.zeros_like(acc_k)
        acc_v[...] = jnp.zeros_like(acc_v)

    @pl.when(step + 1 < steps)
    def _():
        for copy in copies(step + 1, 1 - slot):
            copy.start()

    for copy in copies(step, slot):
        copy.wait()

    enc = rows[slot]
    key_proj = dot(enc, wk_ref[...]).astype(BF16)
    value_proj = dot(enc, wv_ref[...]).astype(BF16)
    for span in range(SPANS_STEP):
        tok = slice(span * span_len, (span + 1) * span_len)
        key = slice(span * keys, (span + 1) * keys)
        for head in range(heads):
            col = slice(head * HEAD_DIM, (head + 1) * HEAD_DIM)
            q, g = q_ref[tok, col], g_ref[tok, col]
            k, v = key_proj[key, col], value_proj[key, col]
            scores = dot(q, k, NT) * scale
            grad_prob = dot(g, v, NT)
            top = jnp.max(scores, axis=-1, keepdims=True)
            weight = jnp.exp(scores - top)
            prob = weight / jnp.sum(weight, axis=-1, keepdims=True)
            prob_round = prob.astype(BF16)
            attended = dot(prob_round, v).astype(BF16)
            att_ref[tok, col] = attended
            delta = jnp.sum(g.astype(F32) * attended.astype(F32), axis=-1, keepdims=True)
            grad_score = (prob * (grad_prob - delta)).astype(BF16)
            gq_ref[tok, col] = (dot(grad_score, k) * scale).astype(BF16)
            gkt[col, key] = (dot(q.T, grad_score) * scale).astype(BF16)
            gvt[col, key] = dot(g.T, prob_round).astype(BF16)
    acc_k[...] += dot(gkt[...], enc)
    acc_v[...] += dot(gvt[...], enc)

    @pl.when(step + 1 == steps)
    def _():
        dwk_ref[...] = acc_k[...].T
        dwv_ref[...] = acc_v[...].T


def attention(ids, database, w_key, w_value, queries, grads, span_len, neighbours):
    key_tokens, enc_width = database.shape[1:]
    features = w_key.shape[1]
    tokens = SPANS_STEP * span_len
    fetched = SPANS_STEP * neighbours
    steps = queries.shape[0] // tokens
    whole = pl.BlockSpec((enc_width, features), lambda i, ids: (0, 0))
    block = pl.BlockSpec((tokens, features), lambda i, ids: (i, 0))
    row_list = pltpu.VMEM((2, fetched * key_tokens, enc_width), BF16)
    total = pltpu.VMEM((features, enc_width), F32)
    grad_t = pltpu.VMEM((features, fetched * key_tokens), BF16)
    flops = 4 * steps * fetched * key_tokens * features * (2 * enc_width + 3 * span_len)
    return pl.pallas_call(
        functools.partial(attention_kernel, span_len, neighbours),
        grid_spec=pltpu.PrefetchScalarGridSpec(
            num_scalar_prefetch=1,
            grid=(steps,),
            in_specs=[pl.BlockSpec(memory_space=pl.ANY), whole, whole, block, block],
            out_specs=[block, block, whole, whole],
            scratch_shapes=[
                row_list,
                total,
                total,
                grad_t,
                grad_t,
                pltpu.SemaphoreType.DMA((2, fetched)),
            ],
        ),
        out_shape=[
            jax.ShapeDtypeStruct(queries.shape, BF16),
            jax.ShapeDtypeStruct(queries.shape, BF16),
            jax.ShapeDtypeStruct((enc_width, features), F32),
            jax.ShapeDtypeStruct((enc_width, features), F32),
        ],
        compiler_params=pltpu.CompilerParams(
            dimension_semantics=("arbitrary",), vmem_limit_bytes=48 * 1024 * 1024
        ),
        cost_estimate=pl.CostEstimate(
            flops=flops, bytes_accessed=24 * 1024 * 1024, transcendentals=1024 * 1024
        ),
    )(ids, database, w_key, w_value, queries, grads)


def sum_over_seq(pair):
    seq_count = lax.axis_size("seq")
    chips = seq_count // 2
    me = lax.axis_index("seq")
    core, chip = lax.rem(me, 2), me // 2
    swap = [(i, i ^ 1) for i in range(seq_count)]
    own = lax.dynamic_index_in_dim(pair, core, 0, keepdims=False)
    other = lax.dynamic_index_in_dim(pair, 1 - core, 0, keepdims=False)
    own = own + lax.ppermute(other, "seq", swap)
    parts = own.reshape(chips, own.shape[0] // chips, own.shape[1])
    part = lax.dynamic_index_in_dim(parts, chip, 0, keepdims=False)
    for away in (1, chips - 1, 2):
        ring = [(i, (i + 2 * away) % seq_count) for i in range(seq_count)]
        there = lax.rem(chip + away, chips)
        part = part + lax.ppermute(
            lax.dynamic_index_in_dim(parts, there, 0, keepdims=False), "seq", ring
        )
    full = jnp.zeros_like(parts)
    full = lax.dynamic_update_index_in_dim(full, part, chip, 0)
    for away in (1, chips - 1, 2):
        ring = [(i, (i + 2 * away) % seq_count) for i in range(seq_count)]
        source = lax.rem(chip + chips - away, chips)
        full = lax.dynamic_update_index_in_dim(full, lax.ppermute(part, "seq", ring), source, 0)
    own = full.reshape(own.shape)
    other = lax.ppermute(own, "seq", swap)
    first = core == 0
    return jnp.where(first, own, other), jnp.where(first, other, own)


def on_device(queries, encoded, w_key, w_value, shard_ids, row_ids, grad_out):
    span_count, neighbours = shard_ids.shape
    shard_rows = encoded.shape[0]
    head_features = w_key.shape[1]
    span_len = queries.shape[0] // span_count
    head_index = lax.axis_index("head")
    share = shard_rows // lax.axis_size("head")
    mine = lax.dynamic_slice_in_dim(encoded, head_index * share, share, 0)
    database = lax.all_gather(mine, ("seq", "head"), axis=0, tiled=True)
    ids = lax.all_gather(shard_ids * shard_rows + row_ids, "head", axis=0, tiled=True).reshape(-1)
    heads_query = lax.all_to_all(queries, "head", split_axis=1, concat_axis=0, tiled=True)
    heads_grad = lax.all_to_all(grad_out, "head", split_axis=1, concat_axis=0, tiled=True)
    attended, grad_query, grad_wkey, grad_wvalue = attention(
        ids, database, w_key, w_value, heads_query, heads_grad, span_len, neighbours
    )
    token_out = lax.all_to_all(attended, "head", split_axis=0, concat_axis=1, tiled=True)
    token_grad = lax.all_to_all(grad_query, "head", split_axis=0, concat_axis=1, tiled=True)
    sum_wkey, sum_wvalue = sum_over_seq(jnp.stack([grad_wkey, grad_wvalue]))
    return (token_out, token_grad, sum_wkey, sum_wvalue)


def solution(mesh):
    return jax.shard_map(
        on_device,
        mesh=mesh,
        in_specs=(
            P(("seq", "head"), None),
            P("seq", None, None),
            P(None, "head"),
            P(None, "head"),
            P(("seq", "head"), None),
            P(("seq", "head"), None),
            P(("seq", "head"), None),
        ),
        out_specs=(
            P(("seq", "head"), None),
            P(("seq", "head"), None),
            P(None, "head"),
            P(None, "head"),
        ),
        check_vma=False,
    )
```

```python
import functools

import jax
import jax.numpy as jnp
from jax import lax
from jax.experimental import pallas as pl
from jax.experimental.pallas import tpu as pltpu
from jax.sharding import PartitionSpec as P

HEAD_DIM = 128
SPANS_STEP = 4
BF16 = jnp.bfloat16
F32 = jnp.float32
NN = (((1,), (0,)), ((), ()))
NT = (((1,), (1,)), ((), ()))


def dot(a, b, dims=NN):
    return lax.dot_general(a, b, dims, preferred_element_type=F32)


def attention_kernel(
    span_len,
    neighbours,
    ids_ref,
    core_ref,
    db_ref,
    wk_ref,
    wv_ref,
    q_ref,
    g_ref,
    out_ref,
    own_ref,
    other_ref,
    rows,
    acc_k,
    acc_v,
    gkt,
    gvt,
    sems,
):
    step, steps = pl.program_id(0), pl.num_programs(0)
    slot = lax.rem(step, 2)
    key_tokens = db_ref.shape[1]
    fetched = SPANS_STEP * neighbours
    keys = neighbours * key_tokens
    features = wk_ref.shape[1]
    heads = features // HEAD_DIM
    scale = HEAD_DIM ** (-0.5)

    def copies(at, into):
        return [
            pltpu.make_async_copy(
                db_ref.at[ids_ref[at * fetched + j]],
                rows.at[into, pl.ds(j * key_tokens, key_tokens)],
                sems.at[into, j],
            )
            for j in range(fetched)
        ]

    @pl.when(step == 0)
    def _():
        for copy in copies(step, slot):
            copy.start()
        acc_k[...] = jnp.zeros_like(acc_k)
        acc_v[...] = jnp.zeros_like(acc_v)

    @pl.when(step + 1 < steps)
    def _():
        for copy in copies(step + 1, 1 - slot):
            copy.start()

    for copy in copies(step, slot):
        copy.wait()

    enc = rows[slot]
    key_proj = dot(enc, wk_ref[...]).astype(BF16)
    value_proj = dot(enc, wv_ref[...]).astype(BF16)
    pairs = [
        (
            slice(span * span_len, (span + 1) * span_len),
            slice(span * keys, (span + 1) * keys),
            slice(head * HEAD_DIM, (head + 1) * HEAD_DIM),
        )
        for span in range(SPANS_STEP)
        for head in range(heads)
    ]
    q = [q_ref[tok, col] for tok, key, col in pairs]
    g = [g_ref[tok, col] for tok, key, col in pairs]
    k = [key_proj[key, col] for tok, key, col in pairs]
    v = [value_proj[key, col] for tok, key, col in pairs]
    scores = [dot(q[i], k[i], NT) * scale for i in range(len(pairs))]
    grad_prob = [dot(g[i], v[i], NT) for i in range(len(pairs))]
    top = [jnp.max(x, axis=-1, keepdims=True) for x in scores]
    weight = [jnp.exp(x - m) for x, m in zip(scores, top)]
    inverse = [1.0 / jnp.sum(x, axis=-1, keepdims=True) for x in weight]
    prob = [x * r for x, r in zip(weight, inverse)]
    prob_round = [x.astype(BF16) for x in prob]
    attended = [dot(prob_round[i], v[i]).astype(BF16) for i in range(len(pairs))]
    delta = [
        jnp.sum(x.astype(F32) * y.astype(F32), axis=-1, keepdims=True)
        for x, y in zip(g, attended)
    ]
    grad_score = [
        (p * (x - d)).astype(BF16) for p, x, d in zip(prob, grad_prob, delta)
    ]
    for i, (tok, key, col) in enumerate(pairs):
        out_ref[tok, col] = attended[i]
        gvt[col, key] = dot(g[i].T, prob_round[i]).astype(BF16)
    for i, (tok, key, col) in enumerate(pairs):
        past = slice(col.start + features, col.stop + features)
        out_ref[tok, past] = (dot(grad_score[i], k[i]) * scale).astype(BF16)
        gkt[col, key] = (dot(q[i].T, grad_score[i]) * scale).astype(BF16)
    acc_k[...] += dot(gkt[...], enc)
    acc_v[...] += dot(gvt[...], enc)

    @pl.when((step + 1 == steps) & (core_ref[0] == 0))
    def _():
        own_ref[...] = acc_k[...].T
        other_ref[...] = acc_v[...].T

    @pl.when((step + 1 == steps) & (core_ref[0] == 1))
    def _():
        own_ref[...] = acc_v[...].T
        other_ref[...] = acc_k[...].T


def attention(ids, core, database, w_key, w_value, inputs, span_len, neighbours):
    key_tokens, enc_width = database.shape[1:]
    features = w_key.shape[1]
    tokens = SPANS_STEP * span_len
    fetched = SPANS_STEP * neighbours
    steps = inputs.shape[0] // tokens
    whole = pl.BlockSpec((enc_width, features), lambda i, ids, core: (0, 0))
    block = [pl.BlockSpec((tokens, features), lambda i, ids, core, j=j: (i, j)) for j in (0, 1)]
    both = pl.BlockSpec((tokens, 2 * features), lambda i, ids, core: (i, 0))
    row_list = pltpu.VMEM((2, fetched * key_tokens, enc_width), BF16)
    total = pltpu.VMEM((features, enc_width), F32)
    grad_t = pltpu.VMEM((features, fetched * key_tokens), BF16)
    flops = 4 * steps * fetched * key_tokens * features * (2 * enc_width + 3 * span_len)
    return pl.pallas_call(
        functools.partial(attention_kernel, span_len, neighbours),
        grid_spec=pltpu.PrefetchScalarGridSpec(
            num_scalar_prefetch=2,
            grid=(steps,),
            in_specs=[pl.BlockSpec(memory_space=pl.ANY), whole, whole, *block],
            out_specs=[both, whole, whole],
            scratch_shapes=[
                row_list,
                total,
                total,
                grad_t,
                grad_t,
                pltpu.SemaphoreType.DMA((2, fetched)),
            ],
        ),
        out_shape=[
            jax.ShapeDtypeStruct(inputs.shape, BF16),
            jax.ShapeDtypeStruct((enc_width, features), F32),
            jax.ShapeDtypeStruct((enc_width, features), F32),
        ],
        compiler_params=pltpu.CompilerParams(
            dimension_semantics=("arbitrary",), vmem_limit_bytes=48 * 1024 * 1024
        ),
        cost_estimate=pl.CostEstimate(
            flops=flops, bytes_accessed=24 * 1024 * 1024, transcendentals=1024 * 1024
        ),
    )(ids, core, database, w_key, w_value, inputs, inputs)


def place_kernel(place_ref, own_ref, other_ref, key_ref, value_ref):
    @pl.when(place_ref[1] == 0)
    def _():
        key_ref[...] = own_ref[0]
        value_ref[...] = other_ref[0]

    @pl.when(place_ref[1] == 1)
    def _():
        key_ref[...] = other_ref[0]
        value_ref[...] = own_ref[0]


def place(chip, core, own, other):
    chips, rows, columns = own.shape
    piece = pl.BlockSpec(
        (1, rows, columns), lambda j, at: (lax.rem(at[0] + chips - j, chips), 0, 0)
    )
    out = pl.BlockSpec((rows, columns), lambda j, at: (j, 0))
    full = jax.ShapeDtypeStruct((chips * rows, columns), F32)
    return pl.pallas_call(
        place_kernel,
        grid_spec=pltpu.PrefetchScalarGridSpec(
            num_scalar_prefetch=1, grid=(chips,), in_specs=[piece, piece], out_specs=[out, out]
        ),
        out_shape=[full, full],
    )(jnp.stack([chip, core]), own, other)


def sum_over_seq(chip, core, own, other):
    seq_count = lax.axis_size("seq")
    chips = seq_count // 2
    swap = [(i, i ^ 1) for i in range(seq_count)]
    rings = [[(i, (i + 2 * away) % seq_count) for i in range(seq_count)] for away in range(chips)]
    own = own + lax.ppermute(other, "seq", swap)
    parts = own.reshape(chips, own.shape[0] // chips, own.shape[1])
    part = lax.dynamic_index_in_dim(parts, chip, 0, keepdims=False)
    for away in range(1, chips):
        there = lax.rem(chip + away, chips)
        given = lax.dynamic_index_in_dim(parts, there, 0, keepdims=False)
        part = part + lax.ppermute(given, "seq", rings[away])
    pieces = [part] + [lax.ppermute(part, "seq", rings[away]) for away in range(1, chips)]
    own = jnp.stack(pieces)
    return place(chip, core, own, lax.ppermute(own, "seq", swap))


def on_device(queries, encoded, w_key, w_value, shard_ids, row_ids, grad_out):
    span_count, neighbours = shard_ids.shape
    shard_rows = encoded.shape[0]
    features = w_key.shape[1]
    tokens = queries.shape[0]
    head_count = lax.axis_size("head")
    head_index, seq_index = lax.axis_index("head"), lax.axis_index("seq")
    chip, core = seq_index // 2, lax.rem(seq_index, 2)
    share = shard_rows // head_count
    mine = lax.dynamic_slice_in_dim(encoded, head_index * share, share, 0)
    database = lax.all_gather(mine, ("seq", "head"), axis=0, tiled=True)
    ids = lax.all_gather(shard_ids * shard_rows + row_ids, "head", axis=0, tiled=True).reshape(-1)
    both = jnp.concatenate(
        [x.reshape(tokens, head_count, features) for x in (queries, grad_out)], axis=2
    )
    inputs = lax.all_to_all(
        both.transpose(1, 0, 2), "head", split_axis=0, concat_axis=0, tiled=True
    )
    outputs, own, other = attention(
        ids,
        core.reshape(1),
        database,
        w_key,
        w_value,
        inputs.reshape(head_count * tokens, 2 * features),
        tokens // span_count,
        neighbours,
    )
    outputs = lax.all_to_all(
        outputs.reshape(inputs.shape), "head", split_axis=0, concat_axis=0, tiled=True
    ).transpose(1, 0, 2)
    sum_wkey, sum_wvalue = sum_over_seq(chip, core, own, other)
    token_out = outputs[:, :, :features].reshape(queries.shape)
    token_grad = outputs[:, :, features:].reshape(queries.shape)
    return (token_out, token_grad, sum_wkey, sum_wvalue)


def solution(mesh):
    return jax.shard_map(
        on_device,
        mesh=mesh,
        in_specs=(
            P(("seq", "head"), None),
            P("seq", None, None),
            P(None, "head"),
            P(None, "head"),
            P(("seq", "head"), None),
            P(("seq", "head"), None),
            P(("seq", "head"), None),
        ),
        out_specs=(
            P(("seq", "head"), None),
            P(("seq", "head"), None),
            P(None, "head"),
            P(None, "head"),
        ),
        check_vma=False,
    )
```

```python
import functools

import jax
import jax.numpy as jnp
from jax import lax
from jax.experimental import pallas as pl
from jax.experimental.pallas import tpu as pltpu
from jax.sharding import PartitionSpec as P

HEAD_DIM = 128
SPANS_STEP = 4
ALONG_Y = 8
BF16 = jnp.bfloat16
F32 = jnp.float32
NN = (((1,), (0,)), ((), ()))
NT = (((1,), (1,)), ((), ()))


def dot(a, b, dims=NN):
    return lax.dot_general(a, b, dims, preferred_element_type=F32)


def attention_kernel(
    span_len,
    neighbours,
    sources,
    source_ref,
    row_ref,
    core_ref,
    *refs,
):
    row_sources, refs = refs[:sources], refs[sources:]
    wk_ref, wv_ref, q_ref, g_ref, out_ref, own_ref, other_ref = refs[:7]
    rows, acc_k, acc_v, gkt, gvt, sems = refs[7:]
    step, steps = pl.program_id(0), pl.num_programs(0)
    slot = lax.rem(step, 2)
    key_tokens = row_sources[0].shape[1]
    fetched = SPANS_STEP * neighbours
    keys = neighbours * key_tokens
    features = wk_ref.shape[1]
    heads = features // HEAD_DIM
    scale = HEAD_DIM ** (-0.5)

    def start(at, into):
        for j in range(fetched):
            source, row = source_ref[at * fetched + j], row_ref[at * fetched + j]
            place = rows.at[into, pl.ds(j * key_tokens, key_tokens)]
            sem = sems.at[into, j]

            def pick(low, high, source=source, row=row, place=place, sem=sem):
                if high - low == 1:
                    pltpu.make_async_copy(row_sources[low].at[row], place, sem).start()
                    return
                middle = (low + high) // 2
                pl.when(source < middle)(functools.partial(pick, low, middle))
                pl.when(source >= middle)(functools.partial(pick, middle, high))

            pick(0, sources)

    @pl.when(step == 0)
    def _():
        start(step, slot)
        acc_k[...] = jnp.zeros_like(acc_k)
        acc_v[...] = jnp.zeros_like(acc_v)

    @pl.when(step + 1 < steps)
    def _():
        start(step + 1, 1 - slot)

    for j in range(fetched):
        place = rows.at[slot, pl.ds(j * key_tokens, key_tokens)]
        pltpu.make_async_copy(row_sources[0].at[0], place, sems.at[slot, j]).wait()

    enc = rows[slot]
    key_proj = dot(enc, wk_ref[...]).astype(BF16)
    value_proj = dot(enc, wv_ref[...]).astype(BF16)
    pairs = [
        (
            slice(span * span_len, (span + 1) * span_len),
            slice(span * keys, (span + 1) * keys),
            slice(head * HEAD_DIM, (head + 1) * HEAD_DIM),
        )
        for span in range(SPANS_STEP)
        for head in range(heads)
    ]
    q_all = q_ref[...].reshape(SPANS_STEP * span_len, features)
    g_all = g_ref[...].reshape(SPANS_STEP * span_len, features)
    q = [q_all[tok, col] for tok, key, col in pairs]
    g = [g_all[tok, col] for tok, key, col in pairs]
    k = [key_proj[key, col] for tok, key, col in pairs]
    v = [value_proj[key, col] for tok, key, col in pairs]
    scores = [dot(q[i], k[i], NT) * scale for i in range(len(pairs))]
    grad_prob = [dot(g[i], v[i], NT) for i in range(len(pairs))]
    top = [jnp.max(x, axis=-1, keepdims=True) for x in scores]
    weight = [jnp.exp(x - m) for x, m in zip(scores, top)]
    inverse = [1.0 / jnp.sum(x, axis=-1, keepdims=True) for x in weight]
    prob = [x * r for x, r in zip(weight, inverse)]
    prob_round = [x.astype(BF16) for x in prob]
    attended = [dot(prob_round[i], v[i]).astype(BF16) for i in range(len(pairs))]
    delta = [
        jnp.sum(x.astype(F32) * y.astype(F32), axis=-1, keepdims=True)
        for x, y in zip(g, attended)
    ]
    grad_score = [
        (p * (x - d)).astype(BF16) for p, x, d in zip(prob, grad_prob, delta)
    ]
    for i, (tok, key, col) in enumerate(pairs):
        out_ref[tok, col] = attended[i]
        gvt[col, key] = dot(g[i].T, prob_round[i]).astype(BF16)
    for i, (tok, key, col) in enumerate(pairs):
        past = slice(col.start + features, col.stop + features)
        out_ref[tok, past] = (dot(grad_score[i], k[i]) * scale).astype(BF16)
        gkt[col, key] = (dot(q[i].T, grad_score[i]) * scale).astype(BF16)
    acc_k[...] += dot(gkt[...], enc)
    acc_v[...] += dot(gvt[...], enc)

    @pl.when((step + 1 == steps) & (core_ref[0] == 0))
    def _():
        own_ref[...] = acc_k[...].T
        other_ref[...] = acc_v[...].T

    @pl.when((step + 1 == steps) & (core_ref[0] == 1))
    def _():
        own_ref[...] = acc_v[...].T
        other_ref[...] = acc_k[...].T


def attention(source, row, core, row_sources, w_key, w_value, inputs, tokens, span_len, neighbours):
    key_tokens, enc_width = row_sources[0].shape[1:]
    features = w_key.shape[1]
    fetched = SPANS_STEP * neighbours
    blocks = SPANS_STEP * span_len // tokens
    steps = inputs.shape[0] // blocks
    whole = pl.BlockSpec((enc_width, features), lambda i, *_: (0, 0))
    block = [pl.BlockSpec((blocks, tokens, features), lambda i, *_, j=j: (i, 0, j)) for j in (0, 1)]
    both = pl.BlockSpec((blocks * tokens, 2 * features), lambda i, *_: (i, 0))
    row_list = pltpu.VMEM((2, fetched * key_tokens, enc_width), BF16)
    total = pltpu.VMEM((features, enc_width), F32)
    grad_t = pltpu.VMEM((features, fetched * key_tokens), BF16)
    flops = 4 * steps * fetched * key_tokens * features * (2 * enc_width + 3 * span_len)
    return pl.pallas_call(
        functools.partial(attention_kernel, span_len, neighbours, len(row_sources)),
        grid_spec=pltpu.PrefetchScalarGridSpec(
            num_scalar_prefetch=3,
            grid=(steps,),
            in_specs=[pl.BlockSpec(memory_space=pl.ANY)] * len(row_sources)
            + [whole, whole, *block],
            out_specs=[both, whole, whole],
            scratch_shapes=[
                row_list,
                total,
                total,
                grad_t,
                grad_t,
                pltpu.SemaphoreType.DMA((2, fetched)),
            ],
        ),
        out_shape=[
            jax.ShapeDtypeStruct((steps * blocks * tokens, 2 * features), BF16),
            jax.ShapeDtypeStruct((enc_width, features), F32),
            jax.ShapeDtypeStruct((enc_width, features), F32),
        ],
        compiler_params=pltpu.CompilerParams(
            dimension_semantics=("arbitrary",), vmem_limit_bytes=48 * 1024 * 1024
        ),
        cost_estimate=pl.CostEstimate(
            flops=flops, bytes_accessed=24 * 1024 * 1024, transcendentals=1024 * 1024
        ),
    )(source, row, core, *row_sources, w_key, w_value, inputs, inputs)


def place_kernel(place_ref, own_ref, other_ref, key_ref, value_ref):
    chips, rows = own_ref.shape[:2]
    for core, (to_own, to_other) in enumerate([(key_ref, value_ref), (value_ref, key_ref)]):

        @pl.when(place_ref[1] == core)
        def _(to_own=to_own, to_other=to_other):
            for away in range(chips):
                at = lax.rem(place_ref[0] + chips - away, chips) * rows
                at = pl.ds(pl.multiple_of(at, rows), rows)
                to_own[at] = own_ref[away]
                to_other[at] = other_ref[away]


def place(chip, core, own, other):
    chips, rows, columns = own.shape
    full = jax.ShapeDtypeStruct((chips * rows, columns), F32)
    vmem = pl.BlockSpec(memory_space=pltpu.VMEM)
    return pl.pallas_call(
        place_kernel,
        in_specs=[pl.BlockSpec(memory_space=pltpu.SMEM), vmem, vmem],
        out_specs=[vmem, vmem],
        out_shape=[full, full],
        compiler_params=pltpu.CompilerParams(vmem_limit_bytes=16 * 1024 * 1024),
    )(jnp.stack([chip, core]), own, other)


def sum_over_seq(chip, core, own, other):
    seq_count = lax.axis_size("seq")
    chips = seq_count // 2
    swap = [(i, i ^ 1) for i in range(seq_count)]
    rings = [[(i, (i + 2 * away) % seq_count) for i in range(seq_count)] for away in range(chips)]
    own = own + lax.ppermute(other, "seq", swap)
    parts = own.reshape(chips, own.shape[0] // chips, own.shape[1])
    part = lax.dynamic_index_in_dim(parts, chip, 0, keepdims=False)
    for away in range(1, chips):
        there = lax.rem(chip + away, chips)
        given = lax.dynamic_index_in_dim(parts, there, 0, keepdims=False)
        part = part + lax.ppermute(given, "seq", rings[away])
    pieces = [part] + [lax.ppermute(part, "seq", rings[away]) for away in range(1, chips)]
    own = jnp.stack(pieces)
    return place(chip, core, own, lax.ppermute(own, "seq", swap))


def gather_rows(encoded, chip, core):
    shard_rows, key_tokens, enc_width = encoded.shape
    head_count, seq_count = lax.axis_size("head"), lax.axis_size("seq")
    half, quarter = shard_rows - ALONG_Y, ALONG_Y // 2
    swap = [(i, i ^ 1) for i in range(seq_count)]
    up = [(i, (i + 2) % seq_count) for i in range(seq_count)]
    down = [(i, (i - 2) % seq_count) for i in range(seq_count)]
    units = encoded[:half].reshape(head_count, half * key_tokens // head_count, enc_width)
    mine = lax.dynamic_index_in_dim(units, lax.axis_index("head"), 0, keepdims=True)
    first = lax.all_gather(mine, ("seq", "head"), axis=0, tiled=True)
    first = first.reshape(seq_count * half, key_tokens, enc_width)
    native = encoded[half:]
    below = lax.ppermute(native, "seq", up)
    above = lax.ppermute(native, "seq", down)
    across_low = lax.ppermute(below[:quarter], "seq", up)
    across_high = lax.ppermute(above[quarter:], "seq", down)
    own = [native, below, above, across_low, across_high]
    return [first] + own + [lax.ppermute(piece, "seq", swap) for piece in own]


def locate(shards, rows, chip, core, shard_rows):
    chips = lax.axis_size("seq") // 2
    half, quarter = shard_rows - ALONG_Y, ALONG_Y // 2
    away = lax.rem(shards // 2 + chips - chip, chips)
    late = rows - half
    piece = jnp.where(away == 0, 0, jnp.where(away == chips - 1, 1, jnp.where(away == 1, 2, 3)))
    piece = jnp.where((away == 2) & (late >= quarter), 4, piece)
    source = 1 + piece + jnp.where(lax.rem(shards, 2) == core, 0, 5)
    row = jnp.where(piece == 4, late - quarter, late)
    return jnp.where(rows < half, 0, source), jnp.where(rows < half, shards * half + rows, row)


def on_device(queries, encoded, w_key, w_value, shard_ids, row_ids, grad_out):
    span_count, neighbours = shard_ids.shape
    shard_rows = encoded.shape[0]
    features = w_key.shape[1]
    tokens = queries.shape[0]
    head_count = lax.axis_size("head")
    seq_index = lax.axis_index("seq")
    chip, core = seq_index // 2, lax.rem(seq_index, 2)
    row_sources = gather_rows(encoded, chip, core)
    both = jnp.concatenate(
        [x.reshape(tokens, head_count, features) for x in (queries, grad_out)], axis=2
    ).transpose(1, 0, 2)
    wanted = (shard_ids * shard_rows + row_ids).reshape(1, 1, -1).astype(BF16)
    wanted = jnp.pad(wanted, ((0, 0), (0, 15), (0, 2 * features - wanted.shape[2])))
    both = jnp.concatenate([both, jnp.broadcast_to(wanted, (head_count,) + wanted.shape[1:])], 1)
    inputs = lax.all_to_all(both, "head", split_axis=0, concat_axis=0, tiled=True)
    ids = inputs[:, tokens, : span_count * neighbours].reshape(-1).astype(jnp.int32)
    source, row = locate(ids // shard_rows, lax.rem(ids, shard_rows), chip, core, shard_rows)
    outputs, own, other = attention(
        source,
        row,
        core.reshape(1),
        row_sources,
        w_key,
        w_value,
        inputs,
        tokens,
        tokens // span_count,
        neighbours,
    )
    outputs = lax.all_to_all(
        outputs.reshape(head_count, tokens, 2 * features),
        "head",
        split_axis=0,
        concat_axis=0,
        tiled=True,
    ).transpose(1, 0, 2)
    sum_wkey, sum_wvalue = sum_over_seq(chip, core, own, other)
    token_out = outputs[:, :, :features].reshape(queries.shape)
    token_grad = outputs[:, :, features:].reshape(queries.shape)
    return (token_out, token_grad, sum_wkey, sum_wvalue)


def solution(mesh):
    return jax.shard_map(
        on_device,
        mesh=mesh,
        in_specs=(
            P(("seq", "head"), None),
            P("seq", None, None),
            P(None, "head"),
            P(None, "head"),
            P(("seq", "head"), None),
            P(("seq", "head"), None),
            P(("seq", "head"), None),
        ),
        out_specs=(
            P(("seq", "head"), None),
            P(("seq", "head"), None),
            P(None, "head"),
            P(None, "head"),
        ),
        check_vma=False,
    )
```

```python
import functools

import jax
import jax.numpy as jnp
from jax import lax
from jax.experimental import pallas as pl
from jax.experimental.pallas import tpu as pltpu
from jax.sharding import PartitionSpec as P

HEAD_DIM = 128
SPANS_STEP = 8
ALONG_Y = 8
BF16 = jnp.bfloat16
F32 = jnp.float32
NN = (((1,), (0,)), ((), ()))
NT = (((1,), (1,)), ((), ()))


def dot(a, b, dims=NN):
    return lax.dot_general(a, b, dims, preferred_element_type=F32)


def attention_kernel(
    span_len,
    neighbours,
    sources,
    source_ref,
    row_ref,
    core_ref,
    *refs,
):
    row_sources, refs = refs[:sources], refs[sources:]
    wk_ref, wv_ref, q_ref, g_ref, out_ref, own_ref, other_ref = refs[:7]
    rows, acc_k, acc_v, gkt, gvt, sems = refs[7:]
    step, steps = pl.program_id(0), pl.num_programs(0)
    slot = lax.rem(step, 2)
    key_tokens = row_sources[0].shape[1]
    fetched = SPANS_STEP * neighbours
    keys = neighbours * key_tokens
    features = wk_ref.shape[1]
    heads = features // HEAD_DIM
    scale = HEAD_DIM ** (-0.5)

    def start(at, into):
        for j in range(fetched):
            source, row = source_ref[at * fetched + j], row_ref[at * fetched + j]
            place = rows.at[into, pl.ds(j * key_tokens, key_tokens)]
            sem = sems.at[into, j]

            def pick(low, high, source=source, row=row, place=place, sem=sem):
                if high - low == 1:
                    pltpu.make_async_copy(row_sources[low].at[row], place, sem).start()
                    return
                middle = (low + high) // 2
                pl.when(source < middle)(functools.partial(pick, low, middle))
                pl.when(source >= middle)(functools.partial(pick, middle, high))

            pick(0, sources)

    @pl.when(step == 0)
    def _():
        start(step, slot)
        acc_k[...] = jnp.zeros_like(acc_k)
        acc_v[...] = jnp.zeros_like(acc_v)

    @pl.when(step + 1 < steps)
    def _():
        start(step + 1, 1 - slot)

    for j in range(fetched):
        place = rows.at[slot, pl.ds(j * key_tokens, key_tokens)]
        pltpu.make_async_copy(row_sources[0].at[0], place, sems.at[slot, j]).wait()

    enc = rows[slot]
    key_proj = dot(enc, wk_ref[...]).astype(BF16)
    value_proj = dot(enc, wv_ref[...]).astype(BF16)
    tokens = SPANS_STEP * span_len
    q_all = q_ref[...].reshape(tokens, features)
    g_all = g_ref[...].reshape(tokens, features)
    at = lax.broadcasted_iota(jnp.int32, (span_len, features), 1) // HEAD_DIM

    def stack(x):
        return jnp.concatenate([jnp.where(at == h, x, jnp.zeros_like(x)) for h in range(heads)])

    def unstack(x):
        parts = [
            x[h * span_len : (h + 1) * span_len, h * HEAD_DIM : (h + 1) * HEAD_DIM]
            for h in range(heads)
        ]
        return jnp.concatenate(parts, axis=1)

    spans = range(SPANS_STEP)
    tok = [slice(i * span_len, (i + 1) * span_len) for i in spans]
    key = [slice(i * keys, (i + 1) * keys) for i in spans]
    q = [stack(q_all[t]) for t in tok]
    g = [stack(g_all[t]) for t in tok]
    k = [key_proj[i] for i in key]
    v = [value_proj[i] for i in key]
    scores = [dot(q[i], k[i], NT) * scale for i in spans]
    grad_prob = [dot(g[i], v[i], NT) for i in spans]
    top = [jnp.max(x, axis=-1, keepdims=True) for x in scores]
    weight = [jnp.exp(x - m) for x, m in zip(scores, top)]
    inverse = [1.0 / jnp.sum(x, axis=-1, keepdims=True) for x in weight]
    prob = [x * r for x, r in zip(weight, inverse)]
    prob_round = [x.astype(BF16) for x in prob]
    attended = [dot(prob_round[i], v[i]).astype(BF16) for i in spans]
    delta = [
        jnp.sum(x.astype(F32) * y.astype(F32), axis=-1, keepdims=True)
        for x, y in zip(g, attended)
    ]
    grad_score = [
        (p * (x - d)).astype(BF16) for p, x, d in zip(prob, grad_prob, delta)
    ]
    for i in spans:
        out_ref[tok[i], :features] = unstack(attended[i])
        gvt[:, key[i]] = dot(g[i].T, prob_round[i]).astype(BF16)
    for i in spans:
        out_ref[tok[i], features:] = unstack((dot(grad_score[i], k[i]) * scale).astype(BF16))
        gkt[:, key[i]] = (dot(q[i].T, grad_score[i]) * scale).astype(BF16)
    acc_k[...] += dot(gkt[...], enc)
    acc_v[...] += dot(gvt[...], enc)

    @pl.when((step + 1 == steps) & (core_ref[0] == 0))
    def _():
        own_ref[...] = acc_k[...].T
        other_ref[...] = acc_v[...].T

    @pl.when((step + 1 == steps) & (core_ref[0] == 1))
    def _():
        own_ref[...] = acc_v[...].T
        other_ref[...] = acc_k[...].T


def attention(source, row, core, row_sources, w_key, w_value, inputs, tokens, span_len, neighbours):
    key_tokens, enc_width = row_sources[0].shape[1:]
    features = w_key.shape[1]
    fetched = SPANS_STEP * neighbours
    blocks = SPANS_STEP * span_len // tokens
    steps = inputs.shape[0] // blocks
    whole = pl.BlockSpec((enc_width, features), lambda i, *_: (0, 0))
    block = [pl.BlockSpec((blocks, tokens, features), lambda i, *_, j=j: (i, 0, j)) for j in (0, 1)]
    both = pl.BlockSpec((blocks * tokens, 2 * features), lambda i, *_: (i, 0))
    row_list = pltpu.VMEM((2, fetched * key_tokens, enc_width), BF16)
    total = pltpu.VMEM((features, enc_width), F32)
    grad_t = pltpu.VMEM((features, fetched * key_tokens), BF16)
    flops = 4 * steps * fetched * key_tokens * features * (2 * enc_width + 3 * span_len)
    return pl.pallas_call(
        functools.partial(attention_kernel, span_len, neighbours, len(row_sources)),
        grid_spec=pltpu.PrefetchScalarGridSpec(
            num_scalar_prefetch=3,
            grid=(steps,),
            in_specs=[pl.BlockSpec(memory_space=pl.ANY)] * len(row_sources)
            + [whole, whole, *block],
            out_specs=[both, whole, whole],
            scratch_shapes=[
                row_list,
                total,
                total,
                grad_t,
                grad_t,
                pltpu.SemaphoreType.DMA((2, fetched)),
            ],
        ),
        out_shape=[
            jax.ShapeDtypeStruct((steps * blocks * tokens, 2 * features), BF16),
            jax.ShapeDtypeStruct((enc_width, features), F32),
            jax.ShapeDtypeStruct((enc_width, features), F32),
        ],
        compiler_params=pltpu.CompilerParams(
            dimension_semantics=("arbitrary",), vmem_limit_bytes=48 * 1024 * 1024
        ),
        cost_estimate=pl.CostEstimate(
            flops=flops, bytes_accessed=24 * 1024 * 1024, transcendentals=1024 * 1024
        ),
    )(source, row, core, *row_sources, w_key, w_value, inputs, inputs)


def place_kernel(place_ref, own_ref, other_ref, key_ref, value_ref):
    chips, rows = own_ref.shape[:2]
    for core, (to_own, to_other) in enumerate([(key_ref, value_ref), (value_ref, key_ref)]):

        @pl.when(place_ref[1] == core)
        def _(to_own=to_own, to_other=to_other):
            for away in range(chips):
                at = lax.rem(place_ref[0] + chips - away, chips) * rows
                at = pl.ds(pl.multiple_of(at, rows), rows)
                to_own[at] = own_ref[away].astype(F32)
                to_other[at] = other_ref[away].astype(F32)


def place(chip, core, own, other):
    chips, rows, columns = own.shape
    full = jax.ShapeDtypeStruct((chips * rows, columns), F32)
    vmem = pl.BlockSpec(memory_space=pltpu.VMEM)
    return pl.pallas_call(
        place_kernel,
        in_specs=[pl.BlockSpec(memory_space=pltpu.SMEM), vmem, vmem],
        out_specs=[vmem, vmem],
        out_shape=[full, full],
        compiler_params=pltpu.CompilerParams(vmem_limit_bytes=16 * 1024 * 1024),
    )(jnp.stack([chip, core]), own, other)


def sum_over_seq(chip, core, own, other):
    seq_count = lax.axis_size("seq")
    chips = seq_count // 2
    swap = [(i, i ^ 1) for i in range(seq_count)]
    rings = [[(i, (i + 2 * away) % seq_count) for i in range(seq_count)] for away in range(chips)]
    own = own + lax.ppermute(other, "seq", swap)
    parts = own.reshape(chips, own.shape[0] // chips, own.shape[1])
    part = lax.dynamic_index_in_dim(parts, chip, 0, keepdims=False)
    for away in range(1, chips):
        there = lax.rem(chip + away, chips)
        given = lax.dynamic_index_in_dim(parts, there, 0, keepdims=False).astype(BF16)
        part = part + lax.ppermute(given, "seq", rings[away]).astype(F32)
    part = part.astype(BF16)
    own = jnp.stack(
        [part] + [lax.ppermute(part, "seq", rings[away]) for away in range(1, chips)]
    )
    return place(chip, core, own, lax.ppermute(own, "seq", swap))


def gather_rows(encoded, chip, core):
    shard_rows, key_tokens, enc_width = encoded.shape
    head_count, seq_count = lax.axis_size("head"), lax.axis_size("seq")
    half, quarter = shard_rows - ALONG_Y, ALONG_Y // 2
    swap = [(i, i ^ 1) for i in range(seq_count)]
    up = [(i, (i + 2) % seq_count) for i in range(seq_count)]
    down = [(i, (i - 2) % seq_count) for i in range(seq_count)]
    units = encoded.reshape(-1, half * key_tokens // head_count, enc_width)
    mine = lax.dynamic_index_in_dim(units, lax.axis_index("head"), 0, keepdims=True)
    first = lax.all_gather(mine, ("seq", "head"), axis=0, tiled=True)
    first = first.reshape(seq_count * half, key_tokens, enc_width)
    native = encoded[half:]
    below = lax.ppermute(native, "seq", up)
    above = lax.ppermute(native, "seq", down)
    across_low = lax.ppermute(below[:quarter], "seq", up)
    across_high = lax.ppermute(above[quarter:], "seq", down)
    own = [native, below, above, across_low, across_high]
    return [first] + own + [lax.ppermute(piece, "seq", swap) for piece in own]


def locate(shards, rows, chip, core, shard_rows):
    chips = lax.axis_size("seq") // 2
    half, quarter = shard_rows - ALONG_Y, ALONG_Y // 2
    away = lax.rem(shards // 2 + chips - chip, chips)
    late = rows - half
    piece = jnp.where(away == 0, 0, jnp.where(away == chips - 1, 1, jnp.where(away == 1, 2, 3)))
    piece = jnp.where((away == 2) & (late >= quarter), 4, piece)
    source = 1 + piece + jnp.where(lax.rem(shards, 2) == core, 0, 5)
    row = jnp.where(piece == 4, late - quarter, late)
    return jnp.where(rows < half, 0, source), jnp.where(rows < half, shards * half + rows, row)


def on_device(queries, encoded, w_key, w_value, shard_ids, row_ids, grad_out):
    span_count, neighbours = shard_ids.shape
    shard_rows = encoded.shape[0]
    features = w_key.shape[1]
    tokens = queries.shape[0]
    head_count = lax.axis_size("head")
    seq_index = lax.axis_index("seq")
    chip, core = seq_index // 2, lax.rem(seq_index, 2)
    row_sources = gather_rows(encoded, chip, core)
    both = jnp.concatenate(
        [x.reshape(tokens, head_count, features) for x in (queries, grad_out)], axis=2
    ).transpose(1, 0, 2)
    wanted = (shard_ids * shard_rows + row_ids).reshape(1, 1, -1).astype(BF16)
    wanted = jnp.pad(wanted, ((0, 0), (0, 15), (0, 2 * features - wanted.shape[2])))
    both = jnp.concatenate([both, jnp.broadcast_to(wanted, (head_count,) + wanted.shape[1:])], 1)
    inputs = lax.all_to_all(both, "head", split_axis=0, concat_axis=0, tiled=True)
    ids = inputs[:, tokens, : span_count * neighbours].reshape(-1).astype(jnp.int32)
    source, row = locate(ids // shard_rows, lax.rem(ids, shard_rows), chip, core, shard_rows)
    outputs, own, other = attention(
        source,
        row,
        core.reshape(1),
        row_sources,
        w_key,
        w_value,
        inputs,
        tokens,
        tokens // span_count,
        neighbours,
    )
    outputs = lax.all_to_all(
        outputs.reshape(head_count, tokens, 2 * features),
        "head",
        split_axis=0,
        concat_axis=0,
        tiled=True,
    ).transpose(1, 0, 2)
    sum_wkey, sum_wvalue = sum_over_seq(chip, core, own, other)
    token_out = outputs[:, :, :features].reshape(queries.shape)
    token_grad = outputs[:, :, features:].reshape(queries.shape)
    return (token_out, token_grad, sum_wkey, sum_wvalue)


def solution(mesh):
    return jax.shard_map(
        on_device,
        mesh=mesh,
        in_specs=(
            P(("seq", "head"), None),
            P("seq", None, None),
            P(None, "head"),
            P(None, "head"),
            P(("seq", "head"), None),
            P(("seq", "head"), None),
            P(("seq", "head"), None),
        ),
        out_specs=(
            P(("seq", "head"), None),
            P(("seq", "head"), None),
            P(None, "head"),
            P(None, "head"),
        ),
        check_vma=False,
    )
```

```python
import functools

import jax
import jax.numpy as jnp
from jax import lax
from jax.experimental import pallas as pl
from jax.experimental.pallas import tpu as pltpu
from jax.sharding import PartitionSpec as P

HEAD_DIM = 128
SPANS_STEP = 8
ALONG_Y = 8
BF16 = jnp.bfloat16
F32 = jnp.float32
NN = (((1,), (0,)), ((), ()))
NT = (((1,), (1,)), ((), ()))


def dot(a, b, dims=NN):
    return lax.dot_general(a, b, dims, preferred_element_type=F32)


def attention_kernel(
    span_len,
    neighbours,
    sources,
    source_ref,
    row_ref,
    core_ref,
    *refs,
):
    row_sources, refs = refs[:sources], refs[sources:]
    wk_ref, wv_ref, q_ref, g_ref, out_ref, own_ref, other_ref = refs[:7]
    rows, acc_k, acc_v, gkt, gvt, sems = refs[7:]
    step, steps = pl.program_id(0), pl.num_programs(0)
    slot = lax.rem(step, 2)
    key_tokens = row_sources[0].shape[1]
    fetched = SPANS_STEP * neighbours
    keys = neighbours * key_tokens
    features = wk_ref.shape[1]
    heads = features // HEAD_DIM
    scale = HEAD_DIM ** (-0.5)

    def start(at, into):
        for j in range(fetched):
            source, row = source_ref[at * fetched + j], row_ref[at * fetched + j]
            place = rows.at[into, pl.ds(j * key_tokens, key_tokens)]
            sem = sems.at[into, j]

            def pick(low, high, source=source, row=row, place=place, sem=sem):
                if high - low == 1:
                    pltpu.make_async_copy(row_sources[low].at[row], place, sem).start()
                    return
                middle = (low + high) // 2
                pl.when(source < middle)(functools.partial(pick, low, middle))
                pl.when(source >= middle)(functools.partial(pick, middle, high))

            pick(0, sources)

    @pl.when(step == 0)
    def _():
        start(step, slot)
        acc_k[...] = jnp.zeros_like(acc_k)
        acc_v[...] = jnp.zeros_like(acc_v)

    @pl.when(step + 1 < steps)
    def _():
        start(step + 1, 1 - slot)

    for j in range(fetched):
        place = rows.at[slot, pl.ds(j * key_tokens, key_tokens)]
        pltpu.make_async_copy(row_sources[0].at[0], place, sems.at[slot, j]).wait()

    enc = rows[slot]
    key_proj = dot(enc, wk_ref[...]).astype(BF16)
    value_proj = dot(enc, wv_ref[...]).astype(BF16)
    tokens = SPANS_STEP * span_len
    q_all = q_ref[...].reshape(tokens, features)
    g_all = g_ref[...].reshape(tokens, features)
    at = lax.broadcasted_iota(jnp.int32, (span_len, features), 1) // HEAD_DIM

    def stack(x):
        return jnp.concatenate([jnp.where(at == h, x, jnp.zeros_like(x)) for h in range(heads)])

    def unstack(x):
        parts = [
            x[h * span_len : (h + 1) * span_len, h * HEAD_DIM : (h + 1) * HEAD_DIM]
            for h in range(heads)
        ]
        return jnp.concatenate(parts, axis=1)

    spans = range(SPANS_STEP)
    tok = [slice(i * span_len, (i + 1) * span_len) for i in spans]
    key = [slice(i * keys, (i + 1) * keys) for i in spans]
    q = [stack(q_all[t]) for t in tok]
    g = [stack(g_all[t]) for t in tok]
    k = [key_proj[i] for i in key]
    v = [value_proj[i] for i in key]
    scores = [dot(q[i], k[i], NT) * scale for i in spans]
    grad_prob = [dot(g[i], v[i], NT) for i in spans]
    top = [jnp.max(x, axis=-1, keepdims=True) for x in scores]
    weight = [jnp.exp(x - m) for x, m in zip(scores, top)]
    inverse = [1.0 / jnp.sum(x, axis=-1, keepdims=True) for x in weight]
    prob = [x * r for x, r in zip(weight, inverse)]
    prob_round = [x.astype(BF16) for x in prob]
    attended = [dot(prob_round[i], v[i]).astype(BF16) for i in spans]
    delta = [
        jnp.sum(x.astype(F32) * y.astype(F32), axis=-1, keepdims=True)
        for x, y in zip(g, attended)
    ]
    grad_score = [
        (p * (x - d)).astype(BF16) for p, x, d in zip(prob, grad_prob, delta)
    ]
    for i in spans:
        out_ref[tok[i], :features] = unstack(attended[i])
        gvt[:, key[i]] = dot(g[i].T, prob_round[i]).astype(BF16)
    for i in spans:
        out_ref[tok[i], features:] = unstack((dot(grad_score[i], k[i]) * scale).astype(BF16))
        gkt[:, key[i]] = (dot(q[i].T, grad_score[i]) * scale).astype(BF16)
    acc_k[...] += dot(gkt[...], enc)
    acc_v[...] += dot(gvt[...], enc)

    @pl.when((step + 1 == steps) & (core_ref[0] == 0))
    def _():
        own_ref[...] = acc_k[...].T
        other_ref[...] = acc_v[...].T

    @pl.when((step + 1 == steps) & (core_ref[0] == 1))
    def _():
        own_ref[...] = acc_v[...].T
        other_ref[...] = acc_k[...].T


def attention(source, row, core, row_sources, w_key, w_value, inputs, tokens, span_len, neighbours):
    key_tokens, enc_width = row_sources[0].shape[1:]
    features = w_key.shape[1]
    fetched = SPANS_STEP * neighbours
    blocks = SPANS_STEP * span_len // tokens
    steps = inputs.shape[0] // blocks
    whole = pl.BlockSpec((enc_width, features), lambda i, *_: (0, 0))
    block = [pl.BlockSpec((blocks, tokens, features), lambda i, *_, j=j: (i, 0, j)) for j in (0, 1)]
    both = pl.BlockSpec((blocks * tokens, 2 * features), lambda i, *_: (i, 0))
    row_list = pltpu.VMEM((2, fetched * key_tokens, enc_width), BF16)
    total = pltpu.VMEM((features, enc_width), F32)
    grad_t = pltpu.VMEM((features, fetched * key_tokens), BF16)
    flops = 4 * steps * fetched * key_tokens * features * (2 * enc_width + 3 * span_len)
    return pl.pallas_call(
        functools.partial(attention_kernel, span_len, neighbours, len(row_sources)),
        grid_spec=pltpu.PrefetchScalarGridSpec(
            num_scalar_prefetch=3,
            grid=(steps,),
            in_specs=[pl.BlockSpec(memory_space=pl.ANY)] * len(row_sources)
            + [whole, whole, *block],
            out_specs=[both, whole, whole],
            scratch_shapes=[
                row_list,
                total,
                total,
                grad_t,
                grad_t,
                pltpu.SemaphoreType.DMA((2, fetched)),
            ],
        ),
        out_shape=[
            jax.ShapeDtypeStruct((steps * blocks * tokens, 2 * features), BF16),
            jax.ShapeDtypeStruct((enc_width, features), F32),
            jax.ShapeDtypeStruct((enc_width, features), F32),
        ],
        compiler_params=pltpu.CompilerParams(
            dimension_semantics=("arbitrary",), vmem_limit_bytes=48 * 1024 * 1024
        ),
        cost_estimate=pl.CostEstimate(
            flops=flops, bytes_accessed=24 * 1024 * 1024, transcendentals=1024 * 1024
        ),
    )(source, row, core, *row_sources, w_key, w_value, inputs, inputs)


def place_kernel(place_ref, own_ref, other_ref, key_ref, value_ref):
    chips, rows = own_ref.shape[:2]
    for core, (to_own, to_other) in enumerate([(key_ref, value_ref), (value_ref, key_ref)]):

        @pl.when(place_ref[1] == core)
        def _(to_own=to_own, to_other=to_other):
            for away in range(chips):
                at = lax.rem(place_ref[0] + chips - away, chips) * rows
                at = pl.ds(pl.multiple_of(at, rows), rows)
                to_own[at] = own_ref[away].astype(F32)
                to_other[at] = other_ref[away].astype(F32)


def place(chip, core, own, other):
    chips, rows, columns = own.shape
    full = jax.ShapeDtypeStruct((chips * rows, columns), F32)
    vmem = pl.BlockSpec(memory_space=pltpu.VMEM)
    return pl.pallas_call(
        place_kernel,
        in_specs=[pl.BlockSpec(memory_space=pltpu.SMEM), vmem, vmem],
        out_specs=[vmem, vmem],
        out_shape=[full, full],
        compiler_params=pltpu.CompilerParams(vmem_limit_bytes=16 * 1024 * 1024),
    )(jnp.stack([chip, core]), own, other)


def sum_over_seq(chip, core, own, other):
    seq_count = lax.axis_size("seq")
    chips = seq_count // 2
    swap = [(i, i ^ 1) for i in range(seq_count)]
    rings = [[(i, (i + 2 * away) % seq_count) for i in range(seq_count)] for away in range(chips)]
    own = own + lax.ppermute(other, "seq", swap)
    parts = own.reshape(chips, own.shape[0] // chips, own.shape[1])
    part = lax.dynamic_index_in_dim(parts, chip, 0, keepdims=False)
    for away in range(1, chips):
        there = lax.rem(chip + away, chips)
        given = lax.dynamic_index_in_dim(parts, there, 0, keepdims=False)
        part = part + lax.ppermute(given, "seq", rings[away])
    part = part.astype(BF16)
    own = jnp.stack(
        [part] + [lax.ppermute(part, "seq", rings[away]) for away in range(1, chips)]
    )
    return place(chip, core, own, lax.ppermute(own, "seq", swap))


def gather_rows(encoded, chip, core):
    shard_rows, key_tokens, enc_width = encoded.shape
    head_count, seq_count = lax.axis_size("head"), lax.axis_size("seq")
    half, quarter = shard_rows - ALONG_Y, ALONG_Y // 2
    swap = [(i, i ^ 1) for i in range(seq_count)]
    up = [(i, (i + 2) % seq_count) for i in range(seq_count)]
    down = [(i, (i - 2) % seq_count) for i in range(seq_count)]
    units = encoded.reshape(-1, half * key_tokens // head_count, enc_width)
    mine = lax.dynamic_index_in_dim(units, lax.axis_index("head"), 0, keepdims=True)
    first = lax.all_gather(mine, ("seq", "head"), axis=0, tiled=True)
    first = first.reshape(seq_count * half, key_tokens, enc_width)
    native = encoded[half:]
    below = lax.ppermute(native, "seq", up)
    above = lax.ppermute(native, "seq", down)
    across_low = lax.ppermute(below[:quarter], "seq", up)
    across_high = lax.ppermute(above[quarter:], "seq", down)
    own = [native, below, above, across_low, across_high]
    return [first] + own + [lax.ppermute(piece, "seq", swap) for piece in own]


def locate(shards, rows, chip, core, shard_rows):
    chips = lax.axis_size("seq") // 2
    half, quarter = shard_rows - ALONG_Y, ALONG_Y // 2
    away = lax.rem(shards // 2 + chips - chip, chips)
    late = rows - half
    piece = jnp.where(away == 0, 0, jnp.where(away == chips - 1, 1, jnp.where(away == 1, 2, 3)))
    piece = jnp.where((away == 2) & (late >= quarter), 4, piece)
    source = 1 + piece + jnp.where(lax.rem(shards, 2) == core, 0, 5)
    row = jnp.where(piece == 4, late - quarter, late)
    return jnp.where(rows < half, 0, source), jnp.where(rows < half, shards * half + rows, row)


def on_device(queries, encoded, w_key, w_value, shard_ids, row_ids, grad_out):
    span_count, neighbours = shard_ids.shape
    shard_rows = encoded.shape[0]
    features = w_key.shape[1]
    tokens = queries.shape[0]
    head_count = lax.axis_size("head")
    seq_index = lax.axis_index("seq")
    chip, core = seq_index // 2, lax.rem(seq_index, 2)
    row_sources = gather_rows(encoded, chip, core)
    both = jnp.concatenate(
        [x.reshape(tokens, head_count, features) for x in (queries, grad_out)], axis=2
    ).transpose(1, 0, 2)
    wanted = (shard_ids * shard_rows + row_ids).reshape(1, 1, -1).astype(BF16)
    wanted = jnp.pad(wanted, ((0, 0), (0, 15), (0, 2 * features - wanted.shape[2])))
    both = jnp.concatenate([both, jnp.broadcast_to(wanted, (head_count,) + wanted.shape[1:])], 1)
    inputs = lax.all_to_all(both, "head", split_axis=0, concat_axis=0, tiled=True)
    ids = inputs[:, tokens, : span_count * neighbours].reshape(-1).astype(jnp.int32)
    source, row = locate(ids // shard_rows, lax.rem(ids, shard_rows), chip, core, shard_rows)
    outputs, own, other = attention(
        source,
        row,
        core.reshape(1),
        row_sources,
        w_key,
        w_value,
        inputs,
        tokens,
        tokens // span_count,
        neighbours,
    )
    outputs = lax.all_to_all(
        outputs.reshape(head_count, tokens, 2 * features),
        "head",
        split_axis=0,
        concat_axis=0,
        tiled=True,
    ).transpose(1, 0, 2)
    sum_wkey, sum_wvalue = sum_over_seq(chip, core, own, other)
    token_out = outputs[:, :, :features].reshape(queries.shape)
    token_grad = outputs[:, :, features:].reshape(queries.shape)
    return (token_out, token_grad, sum_wkey, sum_wvalue)


def solution(mesh):
    return jax.shard_map(
        on_device,
        mesh=mesh,
        in_specs=(
            P(("seq", "head"), None),
            P("seq", None, None),
            P(None, "head"),
            P(None, "head"),
            P(("seq", "head"), None),
            P(("seq", "head"), None),
            P(("seq", "head"), None),
        ),
        out_specs=(
            P(("seq", "head"), None),
            P(("seq", "head"), None),
            P(None, "head"),
            P(None, "head"),
        ),
        check_vma=False,
    )
```

```python
import functools

import jax
import jax.numpy as jnp
from jax import lax
from jax.experimental import pallas as pl
from jax.experimental.pallas import tpu as pltpu
from jax.sharding import PartitionSpec as P

HEAD_DIM = 128
SPANS_STEP = 8
ALONG_Y = 8
BF16 = jnp.bfloat16
F32 = jnp.float32
NN = (((1,), (0,)), ((), ()))
NT = (((1,), (1,)), ((), ()))


def dot(a, b, dims=NN):
    return lax.dot_general(a, b, dims, preferred_element_type=F32)


def attention_kernel(
    span_len,
    neighbours,
    sources,
    source_ref,
    row_ref,
    core_ref,
    *refs,
):
    row_sources, refs = refs[:sources], refs[sources:]
    wk_ref, wv_ref, q_ref, g_ref, out_ref, own_ref, other_ref = refs[:7]
    rows, acc_k, acc_v, gkt, gvt, sems = refs[7:]
    step, steps = pl.program_id(0), pl.num_programs(0)
    slot = lax.rem(step, 2)
    key_tokens = row_sources[0].shape[1]
    fetched = SPANS_STEP * neighbours
    keys = neighbours * key_tokens
    features = wk_ref.shape[1]
    heads = features // HEAD_DIM
    scale = HEAD_DIM ** (-0.5)

    def start(at, into):
        for j in range(fetched):
            source, row = source_ref[at * fetched + j], row_ref[at * fetched + j]
            place = rows.at[into, pl.ds(j * key_tokens, key_tokens)]
            sem = sems.at[into, j]

            def pick(low, high, source=source, row=row, place=place, sem=sem):
                if high - low == 1:
                    pltpu.make_async_copy(row_sources[low].at[row], place, sem).start()
                    return
                middle = (low + high) // 2
                pl.when(source < middle)(functools.partial(pick, low, middle))
                pl.when(source >= middle)(functools.partial(pick, middle, high))

            pick(0, sources)

    @pl.when(step == 0)
    def _():
        start(step, slot)
        acc_k[...] = jnp.zeros_like(acc_k)
        acc_v[...] = jnp.zeros_like(acc_v)

    @pl.when(step + 1 < steps)
    def _():
        start(step + 1, 1 - slot)

    for j in range(fetched):
        place = rows.at[slot, pl.ds(j * key_tokens, key_tokens)]
        pltpu.make_async_copy(row_sources[0].at[0], place, sems.at[slot, j]).wait()

    enc = rows[slot]
    key_proj = dot(enc, wk_ref[...]).astype(BF16)
    value_proj = dot(enc, wv_ref[...]).astype(BF16)
    tokens = SPANS_STEP * span_len
    q_all = q_ref[...].reshape(tokens, features)
    g_all = g_ref[...].reshape(tokens, features)
    at = lax.broadcasted_iota(jnp.int32, (span_len, features), 1) // HEAD_DIM

    def stack(x):
        return jnp.concatenate([jnp.where(at == h, x, jnp.zeros_like(x)) for h in range(heads)])

    def unstack(x):
        parts = [
            x[h * span_len : (h + 1) * span_len, h * HEAD_DIM : (h + 1) * HEAD_DIM]
            for h in range(heads)
        ]
        return jnp.concatenate(parts, axis=1)

    spans = range(SPANS_STEP)
    tok = [slice(i * span_len, (i + 1) * span_len) for i in spans]
    key = [slice(i * keys, (i + 1) * keys) for i in spans]
    q = [stack(q_all[t]) for t in tok]
    g = [stack(g_all[t]) for t in tok]
    k = [key_proj[i] for i in key]
    v = [value_proj[i] for i in key]
    scores = [dot(q[i], k[i], NT) * scale for i in spans]
    grad_prob = [dot(g[i], v[i], NT) for i in spans]
    top = [jnp.max(x, axis=-1, keepdims=True) for x in scores]
    weight = [jnp.exp(x - m) for x, m in zip(scores, top)]
    inverse = [1.0 / jnp.sum(x, axis=-1, keepdims=True) for x in weight]
    prob = [x * r for x, r in zip(weight, inverse)]
    prob_round = [x.astype(BF16) for x in prob]
    attended = [dot(prob_round[i], v[i]).astype(BF16) for i in spans]
    delta = [
        jnp.sum(x.astype(F32) * y.astype(F32), axis=-1, keepdims=True)
        for x, y in zip(g, attended)
    ]
    grad_score = [
        (p * (x - d)).astype(BF16) for p, x, d in zip(prob, grad_prob, delta)
    ]
    for i in spans:
        out_ref[tok[i], :features] = unstack(attended[i])
        gvt[:, key[i]] = dot(g[i].T, prob_round[i]).astype(BF16)
    for i in spans:
        out_ref[tok[i], features:] = unstack((dot(grad_score[i], k[i]) * scale).astype(BF16))
        gkt[:, key[i]] = (dot(q[i].T, grad_score[i]) * scale).astype(BF16)
    acc_k[...] += dot(gkt[...], enc)
    acc_v[...] += dot(gvt[...], enc)

    @pl.when((step + 1 == steps) & (core_ref[0] == 0))
    def _():
        own_ref[...] = acc_k[...].T
        other_ref[...] = acc_v[...].T

    @pl.when((step + 1 == steps) & (core_ref[0] == 1))
    def _():
        own_ref[...] = acc_v[...].T
        other_ref[...] = acc_k[...].T


def attention(source, row, core, row_sources, w_key, w_value, inputs, tokens, span_len, neighbours):
    key_tokens, enc_width = row_sources[0].shape[1:]
    features = w_key.shape[1]
    fetched = SPANS_STEP * neighbours
    blocks = SPANS_STEP * span_len // tokens
    steps = inputs.shape[0] // blocks
    whole = pl.BlockSpec((enc_width, features), lambda i, *_: (0, 0))
    block = [pl.BlockSpec((blocks, tokens, features), lambda i, *_, j=j: (i, 0, j)) for j in (0, 1)]
    both = pl.BlockSpec((blocks * tokens, 2 * features), lambda i, *_: (i, 0))
    row_list = pltpu.VMEM((2, fetched * key_tokens, enc_width), BF16)
    total = pltpu.VMEM((features, enc_width), F32)
    grad_t = pltpu.VMEM((features, fetched * key_tokens), BF16)
    flops = 4 * steps * fetched * key_tokens * features * (2 * enc_width + 3 * span_len)
    return pl.pallas_call(
        functools.partial(attention_kernel, span_len, neighbours, len(row_sources)),
        grid_spec=pltpu.PrefetchScalarGridSpec(
            num_scalar_prefetch=3,
            grid=(steps,),
            in_specs=[pl.BlockSpec(memory_space=pl.ANY)] * len(row_sources)
            + [whole, whole, *block],
            out_specs=[both, whole, whole],
            scratch_shapes=[
                row_list,
                total,
                total,
                grad_t,
                grad_t,
                pltpu.SemaphoreType.DMA((2, fetched)),
            ],
        ),
        out_shape=[
            jax.ShapeDtypeStruct((steps * blocks * tokens, 2 * features), BF16),
            jax.ShapeDtypeStruct((enc_width, features), F32),
            jax.ShapeDtypeStruct((enc_width, features), F32),
        ],
        compiler_params=pltpu.CompilerParams(
            dimension_semantics=("arbitrary",), vmem_limit_bytes=60 * 1024 * 1024
        ),
        cost_estimate=pl.CostEstimate(
            flops=flops, bytes_accessed=24 * 1024 * 1024, transcendentals=1024 * 1024
        ),
    )(source, row, core, *row_sources, w_key, w_value, inputs, inputs)


def place_kernel(place_ref, own_ref, other_ref, key_ref, value_ref):
    chips, rows = own_ref.shape[:2]
    for core, (to_own, to_other) in enumerate([(key_ref, value_ref), (value_ref, key_ref)]):

        @pl.when(place_ref[1] == core)
        def _(to_own=to_own, to_other=to_other):
            for away in range(chips):
                at = lax.rem(place_ref[0] + chips - away, chips) * rows
                at = pl.ds(pl.multiple_of(at, rows), rows)
                to_own[at] = own_ref[away].astype(F32)
                to_other[at] = other_ref[away].astype(F32)


def place(chip, core, own, other):
    chips, rows, columns = own.shape
    full = jax.ShapeDtypeStruct((chips * rows, columns), F32)
    vmem = pl.BlockSpec(memory_space=pltpu.VMEM)
    return pl.pallas_call(
        place_kernel,
        in_specs=[pl.BlockSpec(memory_space=pltpu.SMEM), vmem, vmem],
        out_specs=[vmem, vmem],
        out_shape=[full, full],
        compiler_params=pltpu.CompilerParams(vmem_limit_bytes=16 * 1024 * 1024),
    )(jnp.stack([chip, core]), own, other)


def sum_over_seq(chip, core, own, other):
    seq_count = lax.axis_size("seq")
    chips = seq_count // 2
    swap = [(i, i ^ 1) for i in range(seq_count)]
    rings = [[(i, (i + 2 * away) % seq_count) for i in range(seq_count)] for away in range(chips)]
    halves = [
        x.reshape(chips, x.shape[0] // chips, x.shape[1])
        for x in (own, lax.ppermute(other, "seq", swap))
    ]

    def quarter(at):
        one, two = [lax.dynamic_index_in_dim(x, at, 0, keepdims=False) for x in halves]
        return one + two

    part = quarter(chip)
    for away in range(1, chips):
        part = part + lax.ppermute(quarter(lax.rem(chip + away, chips)), "seq", rings[away])
    part = part.astype(BF16)
    own = jnp.stack(
        [part] + [lax.ppermute(part, "seq", rings[away]) for away in range(1, chips)]
    )
    return place(chip, core, own, lax.ppermute(own, "seq", swap))


def gather_rows(encoded, chip, core):
    shard_rows, key_tokens, enc_width = encoded.shape
    head_count, seq_count = lax.axis_size("head"), lax.axis_size("seq")
    half, quarter = shard_rows - ALONG_Y, ALONG_Y // 2
    swap = [(i, i ^ 1) for i in range(seq_count)]
    up = [(i, (i + 2) % seq_count) for i in range(seq_count)]
    down = [(i, (i - 2) % seq_count) for i in range(seq_count)]
    units = encoded.reshape(-1, half * key_tokens // head_count, enc_width)
    mine = lax.dynamic_index_in_dim(units, lax.axis_index("head"), 0, keepdims=True)
    first = lax.all_gather(mine, ("seq", "head"), axis=0, tiled=True)
    first = first.reshape(seq_count * half, key_tokens, enc_width)
    native = encoded[half:]
    below = lax.ppermute(native, "seq", up)
    above = lax.ppermute(native, "seq", down)
    across_low = lax.ppermute(below[:quarter], "seq", up)
    across_high = lax.ppermute(above[quarter:], "seq", down)
    own = [native, below, above, across_low, across_high]
    return [first] + own + [lax.ppermute(piece, "seq", swap) for piece in own]


def locate(shards, rows, chip, core, shard_rows):
    chips = lax.axis_size("seq") // 2
    half, quarter = shard_rows - ALONG_Y, ALONG_Y // 2
    away = lax.rem(shards // 2 + chips - chip, chips)
    late = rows - half
    piece = jnp.where(away == 0, 0, jnp.where(away == chips - 1, 1, jnp.where(away == 1, 2, 3)))
    piece = jnp.where((away == 2) & (late >= quarter), 4, piece)
    source = 1 + piece + jnp.where(lax.rem(shards, 2) == core, 0, 5)
    row = jnp.where(piece == 4, late - quarter, late)
    return jnp.where(rows < half, 0, source), jnp.where(rows < half, shards * half + rows, row)


def on_device(queries, encoded, w_key, w_value, shard_ids, row_ids, grad_out):
    span_count, neighbours = shard_ids.shape
    shard_rows = encoded.shape[0]
    features = w_key.shape[1]
    tokens = queries.shape[0]
    head_count = lax.axis_size("head")
    seq_index = lax.axis_index("seq")
    chip, core = seq_index // 2, lax.rem(seq_index, 2)
    row_sources = gather_rows(encoded, chip, core)
    both = jnp.concatenate(
        [x.reshape(tokens, head_count, features) for x in (queries, grad_out)], axis=2
    ).transpose(1, 0, 2)
    wanted = (shard_ids * shard_rows + row_ids).reshape(1, 1, -1).astype(BF16)
    wanted = jnp.pad(wanted, ((0, 0), (0, 15), (0, 2 * features - wanted.shape[2])))
    both = jnp.concatenate([both, jnp.broadcast_to(wanted, (head_count,) + wanted.shape[1:])], 1)
    inputs = lax.all_to_all(both, "head", split_axis=0, concat_axis=0, tiled=True)
    ids = inputs[:, tokens, : span_count * neighbours].reshape(-1).astype(jnp.int32)
    source, row = locate(ids // shard_rows, lax.rem(ids, shard_rows), chip, core, shard_rows)
    outputs, own, other = attention(
        source,
        row,
        core.reshape(1),
        row_sources,
        w_key,
        w_value,
        inputs,
        tokens,
        tokens // span_count,
        neighbours,
    )
    outputs = lax.all_to_all(
        outputs.reshape(head_count, tokens, 2 * features),
        "head",
        split_axis=0,
        concat_axis=0,
        tiled=True,
    ).transpose(1, 0, 2)
    sum_wkey, sum_wvalue = sum_over_seq(chip, core, own, other)
    token_out = outputs[:, :, :features].reshape(queries.shape)
    token_grad = outputs[:, :, features:].reshape(queries.shape)
    return (token_out, token_grad, sum_wkey, sum_wvalue)


def solution(mesh):
    return jax.shard_map(
        on_device,
        mesh=mesh,
        in_specs=(
            P(("seq", "head"), None),
            P("seq", None, None),
            P(None, "head"),
            P(None, "head"),
            P(("seq", "head"), None),
            P(("seq", "head"), None),
            P(("seq", "head"), None),
        ),
        out_specs=(
            P(("seq", "head"), None),
            P(("seq", "head"), None),
            P(None, "head"),
            P(None, "head"),
        ),
        check_vma=False,
    )
```

```python
import functools

import jax
import jax.numpy as jnp
from jax import lax
from jax.experimental import pallas as pl
from jax.experimental.pallas import tpu as pltpu
from jax.sharding import PartitionSpec as P

HEAD_DIM = 128
SPANS_STEP = 8
ALONG_Y = 8
BF16 = jnp.bfloat16
F32 = jnp.float32
NN = (((1,), (0,)), ((), ()))
NT = (((1,), (1,)), ((), ()))


def dot(a, b, dims=NN):
    return lax.dot_general(a, b, dims, preferred_element_type=F32)


def attention_kernel(
    span_len,
    neighbours,
    sources,
    source_ref,
    row_ref,
    core_ref,
    *refs,
):
    row_sources, refs = refs[:sources], refs[sources:]
    wk_ref, wv_ref, q_ref, g_ref, out_ref, own_ref, other_ref = refs[:7]
    rows, acc_k, acc_v, gkt, gvt, sems = refs[7:]
    step, steps = pl.program_id(0), pl.num_programs(0)
    slot = lax.rem(step, 2)
    key_tokens = row_sources[0].shape[1]
    fetched = SPANS_STEP * neighbours
    keys = neighbours * key_tokens
    features = wk_ref.shape[1]
    heads = features // HEAD_DIM
    scale = HEAD_DIM ** (-0.5)

    def start(at, into):
        for j in range(fetched):
            source, row = source_ref[at * fetched + j], row_ref[at * fetched + j]
            place = rows.at[into, pl.ds(j * key_tokens, key_tokens)]
            sem = sems.at[into, j]

            def pick(low, high, source=source, row=row, place=place, sem=sem):
                if high - low == 1:
                    pltpu.make_async_copy(row_sources[low].at[row], place, sem).start()
                    return
                middle = (low + high) // 2
                pl.when(source < middle)(functools.partial(pick, low, middle))
                pl.when(source >= middle)(functools.partial(pick, middle, high))

            pick(0, sources)

    @pl.when(step == 0)
    def _():
        start(step, slot)
        acc_k[...] = jnp.zeros_like(acc_k)
        acc_v[...] = jnp.zeros_like(acc_v)

    @pl.when(step + 1 < steps)
    def _():
        start(step + 1, 1 - slot)

    for j in range(fetched):
        place = rows.at[slot, pl.ds(j * key_tokens, key_tokens)]
        pltpu.make_async_copy(row_sources[0].at[0], place, sems.at[slot, j]).wait()

    enc = rows[slot]
    key_proj = dot(enc, wk_ref[...]).astype(BF16)
    value_proj = dot(enc, wv_ref[...]).astype(BF16)
    tokens = SPANS_STEP * span_len
    q_all = q_ref[...].reshape(tokens, features)
    g_all = g_ref[...].reshape(tokens, features)
    at = lax.broadcasted_iota(jnp.int32, (span_len, features), 1) // HEAD_DIM

    def stack(x):
        return jnp.concatenate([jnp.where(at == h, x, jnp.zeros_like(x)) for h in range(heads)])

    def unstack(x):
        parts = [
            x[h * span_len : (h + 1) * span_len, h * HEAD_DIM : (h + 1) * HEAD_DIM]
            for h in range(heads)
        ]
        return jnp.concatenate(parts, axis=1)

    spans = range(SPANS_STEP)
    tok = [slice(i * span_len, (i + 1) * span_len) for i in spans]
    key = [slice(i * keys, (i + 1) * keys) for i in spans]
    q = [stack(q_all[t]) for t in tok]
    g = [stack(g_all[t]) for t in tok]
    k = [key_proj[i] for i in key]
    v = [value_proj[i] for i in key]
    scores = [dot(q[i], k[i], NT) * scale for i in spans]
    grad_prob = [dot(g[i], v[i], NT) for i in spans]
    top = [jnp.max(x, axis=-1, keepdims=True) for x in scores]
    weight = [jnp.exp(x - m) for x, m in zip(scores, top)]
    inverse = [1.0 / jnp.sum(x, axis=-1, keepdims=True) for x in weight]
    prob = [x * r for x, r in zip(weight, inverse)]
    prob_round = [x.astype(BF16) for x in prob]
    attended = [dot(prob_round[i], v[i]).astype(BF16) for i in spans]
    delta = [
        jnp.sum(x.astype(F32) * y.astype(F32), axis=-1, keepdims=True)
        for x, y in zip(g, attended)
    ]
    grad_score = [
        (p * (x - d)).astype(BF16) for p, x, d in zip(prob, grad_prob, delta)
    ]
    for i in spans:
        out_ref[tok[i], :features] = unstack(attended[i])
        gvt[:, key[i]] = dot(g[i].T, prob_round[i]).astype(BF16)
    for i in spans:
        out_ref[tok[i], features:] = unstack((dot(grad_score[i], k[i]) * scale).astype(BF16))
        gkt[:, key[i]] = (dot(q[i].T, grad_score[i]) * scale).astype(BF16)
    acc_k[...] += dot(gkt[...], enc)
    acc_v[...] += dot(gvt[...], enc)

    @pl.when((step + 1 == steps) & (core_ref[0] == 0))
    def _():
        own_ref[...] = acc_k[...].T
        other_ref[...] = acc_v[...].T

    @pl.when((step + 1 == steps) & (core_ref[0] == 1))
    def _():
        own_ref[...] = acc_v[...].T
        other_ref[...] = acc_k[...].T


def attention(source, row, core, row_sources, w_key, w_value, inputs, tokens, span_len, neighbours):
    key_tokens, enc_width = row_sources[0].shape[1:]
    features = w_key.shape[1]
    fetched = SPANS_STEP * neighbours
    blocks = SPANS_STEP * span_len // tokens
    steps = inputs.shape[0] // blocks
    whole = pl.BlockSpec((enc_width, features), lambda i, *_: (0, 0))
    block = [pl.BlockSpec((blocks, tokens, features), lambda i, *_, j=j: (i, 0, j)) for j in (0, 1)]
    both = pl.BlockSpec((blocks * tokens, 2 * features), lambda i, *_: (i, 0))
    row_list = pltpu.VMEM((2, fetched * key_tokens, enc_width), BF16)
    total = pltpu.VMEM((features, enc_width), F32)
    grad_t = pltpu.VMEM((features, fetched * key_tokens), BF16)
    flops = 4 * steps * fetched * key_tokens * features * (2 * enc_width + 3 * span_len)
    return pl.pallas_call(
        functools.partial(attention_kernel, span_len, neighbours, len(row_sources)),
        grid_spec=pltpu.PrefetchScalarGridSpec(
            num_scalar_prefetch=3,
            grid=(steps,),
            in_specs=[pl.BlockSpec(memory_space=pl.ANY)] * len(row_sources)
            + [whole, whole, *block],
            out_specs=[both, whole, whole],
            scratch_shapes=[
                row_list,
                total,
                total,
                grad_t,
                grad_t,
                pltpu.SemaphoreType.DMA((2, fetched)),
            ],
        ),
        out_shape=[
            jax.ShapeDtypeStruct((steps * blocks * tokens, 2 * features), BF16),
            jax.ShapeDtypeStruct((enc_width, features), F32),
            jax.ShapeDtypeStruct((enc_width, features), F32),
        ],
        compiler_params=pltpu.CompilerParams(
            dimension_semantics=("arbitrary",), vmem_limit_bytes=60 * 1024 * 1024
        ),
        cost_estimate=pl.CostEstimate(
            flops=flops, bytes_accessed=24 * 1024 * 1024, transcendentals=1024 * 1024
        ),
    )(source, row, core, *row_sources, w_key, w_value, inputs, inputs)


def place_kernel(place_ref, own_ref, other_ref, key_ref, value_ref):
    chips, rows = own_ref.shape[:2]
    for core, (to_own, to_other) in enumerate([(key_ref, value_ref), (value_ref, key_ref)]):

        @pl.when(place_ref[1] == core)
        def _(to_own=to_own, to_other=to_other):
            for away in range(chips):
                at = lax.rem(place_ref[0] + chips - away, chips) * rows
                at = pl.ds(pl.multiple_of(at, rows), rows)
                to_own[at] = own_ref[away].astype(F32)
                to_other[at] = other_ref[away].astype(F32)


def place(chip, core, own, other):
    chips, rows, columns = own.shape
    full = jax.ShapeDtypeStruct((chips * rows, columns), F32)
    vmem = pl.BlockSpec(memory_space=pltpu.VMEM)
    return pl.pallas_call(
        place_kernel,
        in_specs=[pl.BlockSpec(memory_space=pltpu.SMEM), vmem, vmem],
        out_specs=[vmem, vmem],
        out_shape=[full, full],
        compiler_params=pltpu.CompilerParams(vmem_limit_bytes=16 * 1024 * 1024),
    )(jnp.stack([chip, core]), own, other)


def sum_over_seq(chip, core, own, other):
    seq_count = lax.axis_size("seq")
    chips = seq_count // 2
    swap = [(i, i ^ 1) for i in range(seq_count)]
    rings = [[(i, (i + 2 * away) % seq_count) for i in range(seq_count)] for away in range(chips)]
    halves = [
        x.reshape(chips, x.shape[0] // chips, x.shape[1])
        for x in (own, lax.ppermute(other, "seq", swap))
    ]

    def quarter(at):
        one, two = [lax.dynamic_index_in_dim(x, at, 0, keepdims=False) for x in halves]
        return one + two

    order = sorted(range(1, chips), key=lambda away: -min(away, chips - away))
    part = quarter(chip)
    for away in order:
        part = part + lax.ppermute(quarter(lax.rem(chip + away, chips)), "seq", rings[away])
    part = part.astype(BF16)
    came = {away: lax.ppermute(part, "seq", rings[away]) for away in order}
    own = jnp.stack([part] + [came[away] for away in range(1, chips)])
    return place(chip, core, own, lax.ppermute(own, "seq", swap))


def gather_rows(encoded, chip, core):
    shard_rows, key_tokens, enc_width = encoded.shape
    head_count, seq_count = lax.axis_size("head"), lax.axis_size("seq")
    half, quarter = shard_rows - ALONG_Y, ALONG_Y // 2
    swap = [(i, i ^ 1) for i in range(seq_count)]
    up = [(i, (i + 2) % seq_count) for i in range(seq_count)]
    down = [(i, (i - 2) % seq_count) for i in range(seq_count)]
    unit = half * key_tokens // head_count
    at = lax.axis_index("head") * unit
    mine = lax.dynamic_slice(
        encoded, (at // key_tokens, lax.rem(at, key_tokens), 0), (1, unit, enc_width)
    )
    first = lax.all_gather(mine, ("seq", "head"), axis=0, tiled=True)
    first = first.reshape(seq_count * half, key_tokens, enc_width)
    native = encoded[half:]
    below = lax.ppermute(native, "seq", up)
    above = lax.ppermute(native, "seq", down)
    across_low = lax.ppermute(below[:quarter], "seq", up)
    across_high = lax.ppermute(above[quarter:], "seq", down)
    own = [native, below, above, across_low, across_high]
    return [first] + own + [lax.ppermute(piece, "seq", swap) for piece in own]


def locate(shards, rows, chip, core, shard_rows):
    chips = lax.axis_size("seq") // 2
    half, quarter = shard_rows - ALONG_Y, ALONG_Y // 2
    away = lax.rem(shards // 2 + chips - chip, chips)
    late = rows - half
    piece = jnp.where(away == 0, 0, jnp.where(away == chips - 1, 1, jnp.where(away == 1, 2, 3)))
    piece = jnp.where((away == 2) & (late >= quarter), 4, piece)
    source = 1 + piece + jnp.where(lax.rem(shards, 2) == core, 0, 5)
    row = jnp.where(piece == 4, late - quarter, late)
    return jnp.where(rows < half, 0, source), jnp.where(rows < half, shards * half + rows, row)


def on_device(queries, encoded, w_key, w_value, shard_ids, row_ids, grad_out):
    span_count, neighbours = shard_ids.shape
    shard_rows = encoded.shape[0]
    features = w_key.shape[1]
    tokens = queries.shape[0]
    head_count = lax.axis_size("head")
    seq_index = lax.axis_index("seq")
    chip, core = seq_index // 2, lax.rem(seq_index, 2)
    row_sources = gather_rows(encoded, chip, core)
    both = jnp.concatenate(
        [x.reshape(tokens, head_count, features) for x in (queries, grad_out)], axis=2
    ).transpose(1, 0, 2)
    wanted = (shard_ids * shard_rows + row_ids).reshape(1, 1, -1).astype(BF16)
    wanted = jnp.pad(wanted, ((0, 0), (0, 15), (0, 2 * features - wanted.shape[2])))
    both = jnp.concatenate([both, jnp.broadcast_to(wanted, (head_count,) + wanted.shape[1:])], 1)
    inputs = lax.all_to_all(both, "head", split_axis=0, concat_axis=0, tiled=True)
    ids = inputs[:, tokens, : span_count * neighbours].reshape(-1).astype(jnp.int32)
    source, row = locate(ids // shard_rows, lax.rem(ids, shard_rows), chip, core, shard_rows)
    outputs, own, other = attention(
        source,
        row,
        core.reshape(1),
        row_sources,
        w_key,
        w_value,
        inputs,
        tokens,
        tokens // span_count,
        neighbours,
    )
    outputs = lax.all_to_all(
        outputs.reshape(head_count, tokens, 2 * features),
        "head",
        split_axis=0,
        concat_axis=0,
        tiled=True,
    ).transpose(1, 0, 2)
    sum_wkey, sum_wvalue = sum_over_seq(chip, core, own, other)
    token_out = outputs[:, :, :features].reshape(queries.shape)
    token_grad = outputs[:, :, features:].reshape(queries.shape)
    return (token_out, token_grad, sum_wkey, sum_wvalue)


def solution(mesh):
    return jax.shard_map(
        on_device,
        mesh=mesh,
        in_specs=(
            P(("seq", "head"), None),
            P("seq", None, None),
            P(None, "head"),
            P(None, "head"),
            P(("seq", "head"), None),
            P(("seq", "head"), None),
            P(("seq", "head"), None),
        ),
        out_specs=(
            P(("seq", "head"), None),
            P(("seq", "head"), None),
            P(None, "head"),
            P(None, "head"),
        ),
        check_vma=False,
    )
```
